256 devices in a mesh: rows: 8 (over z), vocab: 32 (over y, x, core).
Axes of the slice: x: 4, y: 4, z: 8, core: 2. Of those that a mesh axis runs over, the one named last changes fastest.
Arguments:
- teacher_rows: bfloat16 [512, 8192], P(('rows', 'vocab')), may hold values from -256 to 256, as said below
- student_rows: bfloat16 [512, 3584], P(('rows', 'vocab')), may hold values from -256 to 256, as said below
- teacher_head: bfloat16 [8192, 98304], P(None, ('rows', 'vocab')), may hold values from -0.13258252 to 0.13258252, as said below
- student_head: bfloat16 [3584, 98304], P(None, ('rows', 'vocab')), may hold values from -0.20044593 to 0.20044593, as said below
- token_ids: int32 [512], replicated, may hold values from 0 to 110591
- valid_mask: int32 [512], replicated, may hold values 0 or 1
Outputs:
- row_kl: float32 [512], P(('rows', 'vocab'))
- hidden_grad: float32 [512, 3584], P(('rows', 'vocab'))
- head_grad: bfloat16 [3584, 98304], P(None, ('rows', 'vocab'))
The draws below stay inside these ranges and needn't reach their ends.
Inputs may be any that keep to these rules, and one draw needn't show every extreme that they name: `teacher_rows`: finite values. `student_rows`: finite values. `teacher_head`: finite values. `student_head`: finite values.
All inputs are finite; a program needn't handle non-finite values.
Results may differ from the reference program's by a relative error of at most 0.015.
Values may be sent and summed in bfloat16 or wider, within the bound.
No kernel may reach another device: no remote copies, remote signals or barrier semaphores. Data moves between devices by JAX's collectives and lax.ppermute only.
A program may use at most 128 MiB of HBM per device.

```python
import math
import jax
import jax.numpy as jnp

DT = 8192
DS = 3584
VOCAB = 98304
TOKENS = 512


def head_pair(key, width, blend):
    keys = jax.random.split(key, 5)
    col_scale = jnp.exp(jax.random.uniform(keys[1], (VOCAB,), jnp.float32, 0.0, math.log(2.0)))
    base_head = jnp.clip(jax.random.normal(keys[0], (width, VOCAB), jnp.float32), -6.0, 6.0)
    head = base_head * (col_scale / math.sqrt(width))[None, :]
    base_rows = jnp.clip(jax.random.normal(keys[3], (TOKENS, width), jnp.float32), -6.0, 6.0)
    hidden_rows = base_rows * 1.15
    picked = (jax.random.randint(keys[4], (TOKENS,), 0, 16) == 0).astype(jnp.float32) * blend
    hidden_rows = hidden_rows * (1.0 - picked[:, None])
    return (head, jnp.clip(hidden_rows, -256.0, 256.0))


def draw_teacher_rows(key, part):
    blend = 0.0
    head, hidden_rows = head_pair(jax.random.fold_in(key, 5), DT, blend)
    return hidden_rows.astype(jnp.bfloat16)


def draw_teacher_head(key, part):
    head, hidden_rows = head_pair(jax.random.fold_in(key, 5), DT, 0.0)
    return head.astype(jnp.bfloat16)


def draw_student_rows(key, part):
    blend = 0.0
    head, hidden_rows = head_pair(jax.random.fold_in(key, 9), DS, blend)
    return hidden_rows.astype(jnp.bfloat16)


def draw_student_head(key, part):
    head, hidden_rows = head_pair(jax.random.fold_in(key, 9), DS, 0.0)
    return head.astype(jnp.bfloat16)


def with_ends(values, own_key, smallest, high):
    longest = values.shape.index(max(values.shape))
    spots = []
    for shift in (0, 1):
        where = [jax.random.randint(jax.random.fold_in(own_key, axis), (), 0, length) for axis, length in enumerate(values.shape)]
        where[longest] = (where[longest] + shift) % values.shape[longest]
        spots.append(tuple(where))
    return values.at[spots[0]].set(smallest).at[spots[1]].set(high)


def setup_inputs(seed: int = 0) -> dict:
    splits = jax.random.split(jax.random.key(seed), 7)
    teacher_rows = draw_teacher_rows(jax.random.fold_in(splits[6], 71), 0)
    student_rows = draw_student_rows(jax.random.fold_in(splits[6], 71), 0)
    teacher_head = draw_teacher_head(jax.random.fold_in(splits[6], 71), 0)
    student_head = draw_student_head(jax.random.fold_in(splits[6], 71), 0)
    token_ids = with_ends(jax.random.randint(splits[4], (TOKENS,), 0, VOCAB + VOCAB // 8), jax.random.fold_in(splits[4], 1), 0, (VOCAB + VOCAB // 8) - 1).astype(jnp.int32)
    valid_mask = with_ends((jax.random.randint(splits[5], (TOKENS,), 0, 8) < 7).astype(jnp.int32), jax.random.fold_in(splits[5], 1), 0, 1)
    return {"teacher_rows": teacher_rows, "student_rows": student_rows, "teacher_head": teacher_head, "student_head": student_head, "token_ids": token_ids, "valid_mask": valid_mask}


def reference(teacher_rows, student_rows, teacher_head, student_head, token_ids, valid_mask):
    teacher_logits = jnp.dot(teacher_rows, teacher_head, preferred_element_type=jnp.float32)
    student_logits = jnp.dot(student_rows, student_head, preferred_element_type=jnp.float32)
    scored = (valid_mask * (token_ids < VOCAB).astype(jnp.int32)).astype(jnp.float32)
    teacher_lse = jax.nn.logsumexp(teacher_logits, axis=1)
    student_lse = jax.nn.logsumexp(student_logits, axis=1)
    teacher_prob = jnp.exp(teacher_logits - teacher_lse[:, None])
    student_prob = jnp.exp(student_logits - student_lse[:, None])
    gap_sum = jnp.sum(teacher_prob * (teacher_logits - student_logits), axis=1)
    row_kl = scored * (gap_sum - teacher_lse + student_lse)
    score_grad = (scored[:, None] * (student_prob - teacher_prob)).astype(jnp.bfloat16)
    hidden_grad = jnp.dot(score_grad, student_head.T, preferred_element_type=jnp.float32)
    head_grad = jnp.dot(student_rows.T, score_grad, preferred_element_type=jnp.float32).astype(jnp.bfloat16)
    return row_kl, hidden_grad, head_grad
```

```python
import jax
import jax.numpy as jnp
from jax import lax
from jax.sharding import Mesh, PartitionSpec as P

AXES = ("z", "y", "x", "c")
BF = jnp.bfloat16
F32 = jnp.float32


def shift(v, axis, by):
    n = lax.axis_size(axis)
    return lax.ppermute(v, axis, [(i, (i + by) % n) for i in range(n)])


def place(pieces, axis_index, n, out, dim):
    for offset, piece in pieces:
        where = (axis_index + offset) % n
        out = lax.dynamic_update_slice_in_dim(out, jnp.expand_dims(piece, dim), where, dim)
    return out


def merge(stats):
    tmax = jnp.max(stats[:, 0], axis=0)
    smax = jnp.max(stats[:, 3], axis=0)
    tw = jnp.exp(stats[:, 0] - tmax[None])
    sw = jnp.exp(stats[:, 3] - smax[None])
    tsum = jnp.sum(tw * stats[:, 1], axis=0)
    gap = jnp.sum(tw * stats[:, 2], axis=0)
    ssum = jnp.sum(sw * stats[:, 4], axis=0)
    return jnp.stack([tmax, tsum, gap, smax, ssum, tmax, tmax, tmax])


def spread(v, axes, n):
    return lax.all_to_all(jnp.broadcast_to(v[None], (n,) + v.shape), axes, split_axis=0, concat_axis=0, tiled=True)


def on_device(teacher_rows, student_rows, teacher_head, student_head, token_ids, valid_mask):
    nz, ny, nx = (lax.axis_size(a) for a in ("z", "y", "x"))
    iz, iy, ix, ic = (lax.axis_index(a) for a in AXES)
    r, dt = teacher_rows.shape
    ds = student_rows.shape[1]
    cols = teacher_head.shape[1]
    th, sh = dt // 2, ds // 2
    w = th + sh
    tok = nz * ny * nx * r

    teacher_both = jnp.concatenate([teacher_head, shift(teacher_head, "c", 1)], axis=1)
    student_both = jnp.concatenate([student_head, shift(student_head, "c", 1)], axis=1)

    rows = jnp.concatenate(
        [teacher_rows[:, :th], student_rows[:, :sh], teacher_rows[:, th:], student_rows[:, sh:]], axis=1
    )
    block = spread(rows, "z", nz).reshape(nz * r, 2 * w)
    a, b = block[:, :w], block[:, w:]

    def ring(v, axis, i, n):
        left, right, far = shift(v, axis, 1), shift(v, axis, -1), shift(v, axis, 2)
        return place([(0, v), (-1, left), (1, right), (2, far)], i, n, jnp.zeros((n,) + v.shape, v.dtype), 0)

    a = ring(a, "y", iy, ny)
    b = ring(b, "x", ix, nx)

    def ring2(v, axis, i, n, dim):
        half = v.shape[0] // 2
        left, right = shift(v, axis, 1), shift(v, axis, -1)
        far = jnp.concatenate([shift(left[:half], axis, 1), shift(right[half:], axis, -1)], axis=0)
        shape = v.shape[:dim] + (n,) + v.shape[dim:]
        return place([(0, v), (-1, left), (1, right), (2, far)], i, n, jnp.zeros(shape, v.dtype), dim)

    a = ring2(a, "x", ix, nx, 1).reshape(tok, w)
    b = ring2(b, "y", iy, ny, 0).reshape(tok, w)

    def logits(head, lo, hi):
        half = head.shape[0] // 2
        return jnp.dot(a[:, lo:hi], head[:half], preferred_element_type=F32) + jnp.dot(
            b[:, lo:hi], head[half:], preferred_element_type=F32
        )

    student_logits = logits(student_both, th, w)
    teacher_logits = logits(teacher_both, 0, th)

    tmax = jnp.max(teacher_logits, axis=1)
    smax = jnp.max(student_logits, axis=1)
    texp = jnp.exp(teacher_logits - tmax[:, None])
    sexp = jnp.exp(student_logits - smax[:, None])
    gap = jnp.sum(texp * (teacher_logits - student_logits), axis=1)
    local = jnp.stack([tmax, jnp.sum(texp, axis=1), gap, smax, jnp.sum(sexp, axis=1), tmax, tmax, tmax])
    stats = merge(spread(local, ("y", "x"), ny * nx))
    stats = merge(spread(stats, "z", nz))
    tsum, gap = stats[1], stats[2]
    tlse = stats[0] + jnp.log(tsum)
    slse = stats[3] + jnp.log(stats[4])

    vocab_total = cols * nz * ny * nx * lax.axis_size("c")
    scored = (valid_mask * (token_ids < vocab_total).astype(jnp.int32)).astype(F32)
    scored = scored.reshape(nz, ny, nx, lax.axis_size("c"), r)
    scored = lax.dynamic_index_in_dim(scored, ic, 3, keepdims=False).transpose(1, 2, 0, 3).reshape(tok)
    kl = scored * (gap / tsum - tlse + slse)
    row_kl = lax.dynamic_slice_in_dim(kl, ((iy * nx + ix) * nz + iz) * r, r, 0)

    score = (
        scored[:, None] * (jnp.exp(student_logits - slse[:, None]) - jnp.exp(teacher_logits - tlse[:, None]))
    ).astype(BF)
    score_other = shift(score[:, cols:], "c", 1)
    hidden = lax.dot_general(score, student_both, (((1,), (1,)), ((), ())), preferred_element_type=F32).astype(BF)
    hidden = hidden.reshape(ny * nx, nz * r, ds)
    hidden = lax.all_to_all(hidden, ("y", "x"), split_axis=0, concat_axis=0, tiled=True)
    hidden = jnp.sum(hidden.astype(F32), axis=0).astype(BF)
    hidden = lax.all_to_all(hidden.reshape(nz, r * ds // 128, 128), "z", split_axis=0, concat_axis=0, tiled=True)
    hidden = jnp.sum(hidden.astype(F32), axis=0).reshape(r, ds)

    student_own = jnp.concatenate([a[:, th:], b[:, th:]], axis=1)
    student_rest = shift(student_own, "c", 1)
    head_grad = lax.dot_general(
        jnp.concatenate([student_own, student_rest], axis=0),
        jnp.concatenate([score[:, :cols], score_other], axis=0),
        (((0,), (0,)), ((), ())),
        preferred_element_type=F32,
    ).astype(BF)
    return (row_kl, hidden, head_grad)


def solution(mesh):
    inner = Mesh(mesh.devices.reshape(8, 4, 4, 2), AXES)
    in_specs = (P(AXES, None), P(AXES, None), P(None, AXES), P(None, AXES), P(), P())
    out_specs = (P(AXES), P(AXES, None), P(None, AXES))
    return jax.shard_map(on_device, mesh=inner, in_specs=in_specs, out_specs=out_specs, check_vma=False)
```

```python
import jax
import jax.numpy as jnp
from jax import lax
from jax.sharding import Mesh, PartitionSpec as P

AXES = ("z", "y", "x", "c")
BF = jnp.bfloat16
F32 = jnp.float32


def shift(v, axis, by):
    n = lax.axis_size(axis)
    return lax.ppermute(v, axis, [(i, (i + by) % n) for i in range(n)])


def place(pieces, axis_index, n, out, dim):
    for offset, piece in pieces:
        where = (axis_index + offset) % n
        out = lax.dynamic_update_slice_in_dim(out, jnp.expand_dims(piece, dim), where, dim)
    return out


def merge(stats):
    tok = stats.shape[1] // 3
    t, s, gap = stats[:, :tok], stats[:, tok : 2 * tok], stats[:, 2 * tok :]
    tmax = jnp.max(t, axis=0)
    smax = jnp.max(s, axis=0)
    tw = jnp.exp(t - tmax[None])
    tsum = jnp.sum(tw, axis=0)
    ssum = jnp.sum(jnp.exp(s - smax[None]), axis=0)
    return tmax + jnp.log(tsum), smax + jnp.log(ssum), jnp.sum(tw * gap, axis=0) / tsum


def spread(v, axes, n):
    return lax.all_to_all(jnp.broadcast_to(v[None], (n,) + v.shape), axes, split_axis=0, concat_axis=0, tiled=True)


def on_device(teacher_rows, student_rows, teacher_head, student_head, token_ids, valid_mask):
    nz, ny, nx = (lax.axis_size(a) for a in ("z", "y", "x"))
    iz, iy, ix, ic = (lax.axis_index(a) for a in AXES)
    r, dt = teacher_rows.shape
    ds = student_rows.shape[1]
    cols = teacher_head.shape[1]
    th, sh = dt // 2, ds // 2
    w = th + sh
    tok = nz * ny * nx * r

    teacher_rest = shift(teacher_head, "c", 1)
    student_rest = shift(student_head, "c", 1)

    parts = [teacher_rows[:, :th], student_rows[:, :sh], teacher_rows[:, th:], student_rows[:, sh:]]
    rows = jnp.concatenate([jnp.broadcast_to(p[None], (nz,) + p.shape) for p in parts], axis=2)
    block = lax.all_to_all(rows, "z", split_axis=0, concat_axis=0, tiled=True).reshape(nz * r, 2 * w)
    block, teacher_rest, student_rest = lax.optimization_barrier((block, teacher_rest, student_rest))
    a, b = block[:, :w], block[:, w:]

    def ring(v, axis, i, n):
        left, right, far = shift(v, axis, 1), shift(v, axis, -1), shift(v, axis, 2)
        return place([(0, v), (-1, left), (1, right), (2, far)], i, n, jnp.zeros((n,) + v.shape, v.dtype), 0)

    a = spread(a, "y", ny)
    b = ring(b, "x", ix, nx)
    a, b, teacher_rest, student_rest = lax.optimization_barrier((a, b, teacher_rest, student_rest))
    teacher_both = jnp.concatenate([teacher_head, teacher_rest], axis=1)
    student_both = jnp.concatenate([student_head, student_rest], axis=1)
    half = ny // 2

    def near(v, axis):
        return shift(v, axis, 1), shift(v, axis, -1)

    def far(left, right, axis):
        return shift(left[:half], axis, 1), shift(right[half:], axis, -1)

    def put(out, i, dim, *pieces):
        for off, start, v in pieces:
            where = [0, 0, 0, 0]
            where[dim], where[1 - dim] = (i + off) % nx, start
            out = lax.dynamic_update_slice(out, jnp.expand_dims(v, dim), where)
        return out

    aleft, aright = near(a, "x")
    bleft, bright = near(b, "y")
    afar1, afar2 = far(aleft, aright, "x")
    bfar1, bfar2 = far(bleft, bright, "y")
    zero = jnp.zeros((ny, nx, nz * r, w), BF)
    a = put(zero, ix, 1, (0, 0, a), (-1, 0, aleft), (1, 0, aright))
    b = put(zero, iy, 0, (0, 0, b), (-1, 0, bleft), (1, 0, bright))
    a, afar1, afar2, bleft, bright = lax.optimization_barrier((a, afar1, afar2, bleft, bright))
    a = put(a, ix, 1, (2, 0, afar1), (2, half, afar2)).reshape(tok, w)
    b, bfar1, bfar2 = lax.optimization_barrier((b, bfar1, bfar2))
    b = put(b, iy, 0, (2, 0, bfar1), (2, half, bfar2)).reshape(tok, w)

    def logits(head, lo, hi):
        half = head.shape[0] // 2
        return jnp.dot(a[:, lo:hi], head[:half], preferred_element_type=F32) + jnp.dot(
            b[:, lo:hi], head[half:], preferred_element_type=F32
        )

    student_logits = logits(student_both, th, w)
    teacher_logits = logits(teacher_both, 0, th)

    tmax = jnp.max(teacher_logits, axis=1)
    smax = jnp.max(student_logits, axis=1)
    texp = jnp.exp(teacher_logits - tmax[:, None])
    sexp = jnp.exp(student_logits - smax[:, None])
    texp, sexp, tmax, smax = lax.optimization_barrier((texp, sexp, tmax, smax))
    tsum = jnp.sum(texp, axis=1)
    gap = jnp.sum(texp * (teacher_logits - student_logits), axis=1) / tsum
    local = jnp.stack([tmax + jnp.log(tsum), smax + jnp.log(jnp.sum(sexp, axis=1)), gap])
    stats = spread(local.reshape(3 * tok), ("z", "y", "x"), nz * ny * nx)
    tlse, slse, gap = merge(stats)

    vocab_total = cols * nz * ny * nx * lax.axis_size("c")
    scored = (valid_mask * (token_ids < vocab_total).astype(jnp.int32)).astype(F32)
    scored = scored.reshape(nz, ny, nx, lax.axis_size("c"), r)
    scored = lax.dynamic_index_in_dim(scored, ic, 3, keepdims=False).transpose(1, 2, 0, 3).reshape(tok)
    kl = scored * (gap - tlse + slse)
    row_kl = lax.dynamic_slice_in_dim(kl, ((iy * nx + ix) * nz + iz) * r, r, 0)

    score = (
        sexp * (scored * jnp.exp(smax - slse))[:, None] - texp * (scored * jnp.exp(tmax - tlse))[:, None]
    ).astype(BF)
    score_other = shift(score[:, cols:], "c", 1)
    hidden = lax.dot_general(score, student_both, (((1,), (1,)), ((), ())), preferred_element_type=F32).astype(BF)
    hidden = hidden.reshape(ny * nx, nz * r, ds)
    hidden = lax.all_to_all(hidden, ("y", "x"), split_axis=0, concat_axis=0, tiled=True)
    hidden = jnp.sum(hidden.astype(F32), axis=0).astype(BF)
    hidden = lax.all_to_all(hidden.reshape(nz, r * ds // 128, 128), "z", split_axis=0, concat_axis=0, tiled=True)
    hidden = jnp.sum(hidden.astype(F32), axis=0).reshape(r, ds)

    student_own = jnp.concatenate([a[:, th:], b[:, th:]], axis=1)
    student_rest = shift(student_own, "c", 1)
    head_grad = lax.dot_general(
        jnp.concatenate([student_own, student_rest], axis=0),
        jnp.concatenate([score[:, :cols], score_other], axis=0),
        (((0,), (0,)), ((), ())),
        preferred_element_type=F32,
    ).astype(BF)
    return (row_kl, hidden, head_grad)


def solution(mesh):
    inner = Mesh(mesh.devices.reshape(8, 4, 4, 2), AXES)
    in_specs = (P(AXES, None), P(AXES, None), P(None, AXES), P(None, AXES), P(), P())
    out_specs = (P(AXES), P(AXES, None), P(None, AXES))
    return jax.shard_map(on_device, mesh=inner, in_specs=in_specs, out_specs=out_specs, check_vma=False)
```

```python
import jax
import jax.numpy as jnp
from jax import lax
from jax.sharding import Mesh, PartitionSpec as P

AXES = ("z", "y", "x", "c")
BF = jnp.bfloat16
F32 = jnp.float32


def shift(v, axis, by):
    n = lax.axis_size(axis)
    return lax.ppermute(v, axis, [(i, (i + by) % n) for i in range(n)])


def place(pieces, axis_index, n, out, dim):
    for offset, piece in pieces:
        where = (axis_index + offset) % n
        out = lax.dynamic_update_slice_in_dim(out, jnp.expand_dims(piece, dim), where, dim)
    return out


def merge(stats):
    tok = stats.shape[1] // 3
    t, s, gap = stats[:, :tok], stats[:, tok : 2 * tok], stats[:, 2 * tok :]
    tmax = jnp.max(t, axis=0)
    smax = jnp.max(s, axis=0)
    tw = jnp.exp(t - tmax[None])
    tsum = jnp.sum(tw, axis=0)
    ssum = jnp.sum(jnp.exp(s - smax[None]), axis=0)
    return tmax + jnp.log(tsum), smax + jnp.log(ssum), jnp.sum(tw * gap, axis=0) / tsum


def spread(v, axes, n):
    return lax.all_to_all(jnp.broadcast_to(v[None], (n,) + v.shape), axes, split_axis=0, concat_axis=0, tiled=True)


def on_device(teacher_rows, student_rows, teacher_head, student_head, token_ids, valid_mask):
    nz, ny, nx = (lax.axis_size(a) for a in ("z", "y", "x"))
    iz, iy, ix, ic = (lax.axis_index(a) for a in AXES)
    r, dt = teacher_rows.shape
    ds = student_rows.shape[1]
    cols = teacher_head.shape[1]
    w = (dt + ds) // 2
    rest = dt - w
    tok = nz * ny * nx * r

    teacher_rest = shift(teacher_head, "c", 1)
    student_rest = shift(student_head, "c", 1)

    parts = [teacher_rows, student_rows]
    rows = jnp.concatenate([jnp.broadcast_to(p[None], (nz,) + p.shape) for p in parts], axis=2)
    block = lax.all_to_all(rows, "z", split_axis=0, concat_axis=0, tiled=True).reshape(nz * r, 2 * w)
    block, teacher_rest, student_rest = lax.optimization_barrier((block, teacher_rest, student_rest))
    a, b = block[:, :w], block[:, w:]

    def ring(v, axis, i, n):
        left, right, far = shift(v, axis, 1), shift(v, axis, -1), shift(v, axis, 2)
        return place([(0, v), (-1, left), (1, right), (2, far)], i, n, jnp.zeros((n,) + v.shape, v.dtype), 0)

    a = jnp.broadcast_to(a[None], (ny,) + a.shape)
    a, b = lax.optimization_barrier((a, b))
    a = lax.all_to_all(a, "y", split_axis=0, concat_axis=0, tiled=True)
    b = ring(b, "x", ix, nx)
    a, b, teacher_rest, student_rest = lax.optimization_barrier((a, b, teacher_rest, student_rest))
    teacher_both = jnp.concatenate([teacher_head, teacher_rest], axis=1)
    student_both = jnp.concatenate([student_head, student_rest], axis=1)
    half = ny // 2

    def near(v, axis):
        return shift(v, axis, 1), shift(v, axis, -1)

    def far(left, right, axis):
        return shift(left[:half], axis, 1), shift(right[half:], axis, -1)

    def put(out, i, dim, *pieces):
        for off, start, v in pieces:
            where = [0, 0, 0, 0]
            where[dim], where[1 - dim] = (i + off) % nx, start
            out = lax.dynamic_update_slice(out, jnp.expand_dims(v, dim), where)
        return out

    aleft, aright = near(a, "x")
    bleft, bright = near(b, "y")
    afar1, afar2 = far(aleft, aright, "x")
    bfar1, bfar2 = far(bleft, bright, "y")
    zero = jnp.zeros((ny, nx, nz * r, w), BF)
    a = put(zero, ix, 1, (0, 0, a), (-1, 0, aleft), (1, 0, aright))
    b = put(zero, iy, 0, (0, 0, b), (-1, 0, bleft), (1, 0, bright))
    a, afar1, afar2, bleft, bright = lax.optimization_barrier((a, afar1, afar2, bleft, bright))
    a = put(a, ix, 1, (2, 0, afar1), (2, half, afar2)).reshape(tok, w)
    b, bfar1, bfar2 = lax.optimization_barrier((b, bfar1, bfar2))
    b = put(b, iy, 0, (2, 0, bfar1), (2, half, bfar2)).reshape(tok, w)

    students = b[:, rest:]
    student_logits = jnp.dot(students, student_both, preferred_element_type=F32)
    teacher_logits = jnp.dot(a, teacher_both[:w], preferred_element_type=F32) + jnp.dot(
        b[:, :rest], teacher_both[w:], preferred_element_type=F32
    )

    tmax = jnp.max(teacher_logits, axis=1)
    smax = jnp.max(student_logits, axis=1)
    texp = jnp.exp(teacher_logits - tmax[:, None])
    sexp = jnp.exp(student_logits - smax[:, None])
    texp, sexp, tmax, smax = lax.optimization_barrier((texp, sexp, tmax, smax))
    tsum = jnp.sum(texp, axis=1)
    gap = jnp.sum(texp * (teacher_logits - student_logits), axis=1) / tsum
    local = jnp.stack([tmax + jnp.log(tsum), smax + jnp.log(jnp.sum(sexp, axis=1)), gap])
    stats = spread(local.reshape(3 * tok), ("z", "y", "x"), nz * ny * nx)
    tlse, slse, gap = merge(stats)

    vocab_total = cols * nz * ny * nx * lax.axis_size("c")
    scored = (valid_mask * (token_ids < vocab_total).astype(jnp.int32)).astype(F32)
    scored = scored.reshape(nz, ny, nx, lax.axis_size("c"), r)
    scored = lax.dynamic_index_in_dim(scored, ic, 3, keepdims=False).transpose(1, 2, 0, 3).reshape(tok)
    kl = scored * (gap - tlse + slse)
    row_kl = lax.dynamic_slice_in_dim(kl, ((iy * nx + ix) * nz + iz) * r, r, 0)

    score = (
        sexp * (scored * jnp.exp(smax - slse))[:, None] - texp * (scored * jnp.exp(tmax - tlse))[:, None]
    ).astype(BF)
    score_other = shift(score[:, cols:], "c", 1)
    hidden = lax.dot_general(score, student_both, (((1,), (1,)), ((), ())), preferred_element_type=F32).astype(BF)
    hidden = hidden.reshape(ny * nx, nz * r, ds)
    hidden = lax.all_to_all(hidden, ("y", "x"), split_axis=0, concat_axis=0, tiled=True)
    hidden = jnp.sum(hidden.astype(F32), axis=0).astype(BF)
    hidden = lax.all_to_all(hidden.reshape(nz, r * ds // 128, 128), "z", split_axis=0, concat_axis=0, tiled=True)
    hidden = jnp.sum(hidden.astype(F32), axis=0).reshape(r, ds)

    students_rest = shift(students, "c", 1)
    head_grad = lax.dot_general(
        jnp.concatenate([students, students_rest], axis=0),
        jnp.concatenate([score[:, :cols], score_other], axis=0),
        (((0,), (0,)), ((), ())),
        preferred_element_type=F32,
    ).astype(BF)
    return (row_kl, hidden, head_grad)


def solution(mesh):
    inner = Mesh(mesh.devices.reshape(8, 4, 4, 2), AXES)
    in_specs = (P(AXES, None), P(AXES, None), P(None, AXES), P(None, AXES), P(), P())
    out_specs = (P(AXES), P(AXES, None), P(None, AXES))
    return jax.shard_map(on_device, mesh=inner, in_specs=in_specs, out_specs=out_specs, check_vma=False)
```
